128 devices in a mesh: dp: 16 (over x, z_lo, core), vocab: 8 (over y, z_hi).
Axes of the slice: x: 4, y: 4, z: 4 (z_hi: 2, z_lo: 2; z = z_hi * 2 + z_lo), core: 2. Of those that a mesh axis runs over, the one named last changes fastest.
Arguments:
- hidden_states: bfloat16 [32768, 4096], P('dp'), may hold values from -6 to 6
- logit_grads: bfloat16 [32768, 12288], P('dp', 'vocab'), may hold values from -0.03125 to 0.03125
- master: float32 [8, 1536, 4096], P('vocab', 'dp'), may hold values from -0.006 to 0.006
- moment_one: float32 [8, 1536, 4096], P('vocab', 'dp'), may hold values from -4 to 4
- moment_two: float32 [8, 1536, 4096], P('vocab', 'dp'), may hold values from 0.0001 to 0.01
Outputs:
- new_master: float32 [8, 1536, 4096], P('vocab', 'dp')
- new_moment_one: float32 [8, 1536, 4096], P('vocab', 'dp')
- new_moment_two: float32 [8, 1536, 4096], P('vocab', 'dp')
- sampler_head: bfloat16 [12288, 4096], P(None, 'vocab')
The draws below stay inside these ranges and needn't reach their ends.
All inputs are finite; a program needn't handle non-finite values.
Results may differ from the reference program's by a relative error of at most 0.001.
Values may be sent and summed in bfloat16 or wider, within the bound.
No kernel may reach another device: no remote copies, remote signals or barrier semaphores. Data moves between devices by JAX's collectives and lax.ppermute only.
A program may use at most 192 MiB of HBM per device.

```python
import math
import jax
import jax.numpy as jnp

D = 4096
STEP = 100
SHARD_ROWS = 1536
VB = 12288
TOKENS = 32768
N_VOCAB = 8


def shard_levels(rng, extent, pieces, smallest, largest):
    gain, own = 1.0, jax.random.fold_in(rng, 6)
    for axis_at, shards_of in pieces:
        heights = jnp.exp(jax.random.uniform(jax.random.fold_in(own, axis_at), (shards_of,), jnp.float32, smallest / len(pieces), largest / len(pieces)))
        gain = gain * jnp.repeat(heights, extent[axis_at] // shards_of).reshape([-1 if axis == axis_at else 1 for axis in range(len(extent))])
    return gain


def normal_values(stream_key, extent, width, limit, pieces=(), kind=jnp.bfloat16):
    loudness = shard_levels(stream_key, extent, pieces, -0.22, 0.18) if pieces else 1.0
    values = jax.random.normal(stream_key, extent, jnp.float32) * width * loudness
    return jnp.minimum(jnp.maximum(values, -limit), limit).astype(kind)


def setup_inputs(seed: int = 0) -> dict:
    streams_of = jax.random.split(jax.random.key(seed), 6)
    hidden_states = normal_values(streams_of[0], (TOKENS, D), 1.0, 6.0, ((0, 16),))
    logit_grads = normal_values(streams_of[1], (TOKENS, VB), TOKENS ** -0.5, 0.03125, ((0, 16), (1, 8)))
    master = normal_values(streams_of[2], (N_VOCAB, SHARD_ROWS, D), 0.001, 0.006, ((0, 8), (1, 16)), jnp.float32)
    moment_one = normal_values(streams_of[3], (N_VOCAB, SHARD_ROWS, D), 0.3, 4.0, ((0, 8), (1, 16)), jnp.float32)
    moment_two = jnp.clip(jnp.exp(math.log(0.01) - 4.6051702 * jax.random.uniform(streams_of[4], (N_VOCAB, SHARD_ROWS, D), jnp.float32) ** shard_levels(streams_of[4], (N_VOCAB, SHARD_ROWS, D), ((0, 8), (1, 16)), -0.2, 0.2)), 0.0001, 0.01)
    return dict(hidden_states=hidden_states, logit_grads=logit_grads, master=master, moment_one=moment_one, moment_two=moment_two)


beta_one = 0.9
beta_two = 0.999
learn_rate = 0.001
decay_rate = 0.1
epsilon = 1e-08

def reference(hidden_states, logit_grads, master, moment_one, moment_two):
    gradient = jnp.dot(logit_grads.T, hidden_states, preferred_element_type=jnp.float32)
    gradient = gradient.reshape(N_VOCAB, SHARD_ROWS, D)
    new_moment_one = beta_one * moment_one + (1.0 - beta_one) * gradient
    new_moment_two = beta_two * moment_two + (1.0 - beta_two) * gradient * gradient
    first_hat = new_moment_one / (1.0 - beta_one ** STEP)
    second_hat = new_moment_two / (1.0 - beta_two ** STEP)
    new_master = master - learn_rate * (first_hat / (jnp.sqrt(second_hat) + epsilon) + decay_rate * master)
    sampler_head = new_master.astype(jnp.bfloat16).reshape(VB, D)
    return (new_master, new_moment_one, new_moment_two, sampler_head)
```

```python
import jax
import jax.numpy as jnp
import numpy as np
from jax import lax
from jax.experimental import pallas as pl
from jax.experimental.pallas import tpu as pltpu
from jax.sharding import Mesh, PartitionSpec as P

STEP = 100

beta_one = 0.9
beta_two = 0.999
learn_rate = 0.001
decay_rate = 0.1
epsilon = 1e-08

F16 = jnp.float16
F32 = jnp.float32
BF16 = jnp.bfloat16
PARAMS = pltpu.CompilerParams(vmem_limit_bytes=48 * 2**20)

SWAP = [(0, 1), (1, 0)]
UP = [(i, (i + 1) % 4) for i in range(4)]
DOWN = [(i, (i + 3) % 4) for i in range(4)]

ROWS = 48
COLS = 256


def order_kernel(slot, grads, out):
    turned = grads[...].T
    for q in range(8):
        at = pl.multiple_of(slot[pl.program_id(0) * 8 + q] * 16, 16)
        out[pl.ds(at, 16), :] = turned[16 * q : 16 * q + 16]


def order_rows(slot, logit_grads):
    return pl.pallas_call(
        order_kernel,
        grid_spec=pltpu.PrefetchScalarGridSpec(
            num_scalar_prefetch=1,
            grid=(12,),
            in_specs=[pl.BlockSpec((2048, 128), lambda i, s: (0, i))],
            out_specs=pl.BlockSpec((1536, 2048), lambda i, s: (0, 0)),
        ),
        out_shape=jax.ShapeDtypeStruct((1536, 2048), BF16),
        compiler_params=PARAMS,
        name="order_rows",
    )(slot, logit_grads)


def product_kernel(rows, hidden, out):
    out[...] = jnp.dot(rows[...], hidden[...], preferred_element_type=F32)


def product(rows, hidden, part, half):
    return pl.pallas_call(
        product_kernel,
        grid=(8,),
        in_specs=[
            pl.BlockSpec((384, 2048), lambda w: (part, 0)),
            pl.BlockSpec((2048, COLS), lambda w: (0, 2 * w + half)),
        ],
        out_specs=pl.BlockSpec((384, COLS), lambda w: (0, w)),
        out_shape=jax.ShapeDtypeStruct((384, 8 * COLS), F32),
        compiler_params=PARAMS,
        cost_estimate=pl.CostEstimate(
            flops=2 * 384 * 2048 * 8 * COLS, bytes_accessed=13 * 2**20, transcendentals=0
        ),
        name=f"product_{part}_{half}",
    )(rows, hidden)


def adam_kernel(first_chunk, gradient, master, one, two, *rest):
    new_master, new_one, new_two, rounded = rest if first_chunk else rest[3:]
    g = gradient[...]
    m = beta_one * one[...] + (1.0 - beta_one) * g
    v = beta_two * two[...] + (1.0 - beta_two) * g * g
    first_hat = m / (1.0 - beta_one**STEP)
    second_hat = v / (1.0 - beta_two**STEP)
    old = master[...]
    new = old - learn_rate * (first_hat / (jnp.sqrt(second_hat) + epsilon) + decay_rate * old)
    new_master[...] = new
    new_one[...] = m
    new_two[...] = v
    rounded[...] = new.astype(BF16)[None]


def adam(gradient, state, outs, part, half):
    tile = pl.BlockSpec((ROWS, COLS), lambda w: (part, 2 * w + half))
    whole = pl.BlockSpec(memory_space=pl.ANY)
    given = () if outs is None else outs
    got = pl.pallas_call(
        lambda *refs: adam_kernel(outs is None, *refs),
        grid=(8,),
        in_specs=[pl.BlockSpec((ROWS, COLS), lambda w: (0, w)), tile, tile, tile] + [whole] * len(given),
        out_specs=[tile] * 3 + [pl.BlockSpec((1, ROWS, COLS), lambda w: (w, 0, 0))],
        out_shape=[jax.ShapeDtypeStruct((96, 4096), F32)] * 3 + [jax.ShapeDtypeStruct((8, ROWS, COLS), BF16)],
        input_output_aliases={} if outs is None else {4: 0, 5: 1, 6: 2},
        compiler_params=PARAMS,
        name=f"adam_{part}_{half}",
    )(gradient, *state, *given)
    return got[:3], got[3]


def place_kernel(first_chunk, dp, own, other, *rest):
    out = rest[-1]

    @pl.when(pl.program_id(0) == 0)
    def _():
        out[...] = own[...].reshape(out.shape)

    @pl.when(pl.program_id(0) == 1)
    def _():
        out[...] = other[...].reshape(out.shape)


def place(dp, own, other, head, part, half):
    given = () if head is None else (head,)
    return pl.pallas_call(
        lambda *refs: place_kernel(head is None, *refs),
        grid_spec=pltpu.PrefetchScalarGridSpec(
            num_scalar_prefetch=1,
            grid=(2, 8),
            in_specs=[
                pl.BlockSpec((1, 8, ROWS, COLS), lambda c, i, s: (jnp.where(c == 0, i, 7), 0, 0, 0)),
                pl.BlockSpec((1, 8, ROWS, COLS), lambda c, i, s: (jnp.where(c == 0, 0, i), 0, 0, 0)),
            ]
            + [pl.BlockSpec(memory_space=pl.ANY)] * len(given),
            out_specs=pl.BlockSpec((8, 1, ROWS, COLS), lambda c, i, s: (0, s[c * 8 + i], part, half)),
        ),
        out_shape=jax.ShapeDtypeStruct((8, 16, 96, 512), BF16),
        input_output_aliases={} if head is None else {3: 0},
        compiler_params=PARAMS,
        name=f"place_{part}_{half}",
    )(dp, own.reshape(8, 8, ROWS, COLS), other.reshape(8, 8, ROWS, COLS), *given)


def wide(a):
    return a.astype(F32)


def ring_sum(parts):
    to_up = lax.ppermute(parts(2, 0).astype(F16), "x", UP)
    to_down = lax.ppermute(parts(2, 1).astype(F16), "x", DOWN)
    up = jnp.concatenate([parts(1, 0) + wide(to_up), parts(1, 1)], 0).astype(F16)
    down = jnp.concatenate([parts(3, 0), parts(3, 1) + wide(to_down)], 0).astype(F16)
    from_down = lax.ppermute(up, "x", UP)
    from_up = lax.ppermute(down, "x", DOWN)
    own = jnp.concatenate([parts(0, 0), parts(0, 1)], 0)
    return own + wide(from_down) + wide(from_up)


def ring_gather(own):
    n = own.shape[0] // 2
    below = lax.ppermute(own, "x", UP)
    above = lax.ppermute(own, "x", DOWN)
    far_low = lax.ppermute(below[:n], "x", UP)
    far_high = lax.ppermute(above[n:], "x", DOWN)
    return jnp.stack([own, above, jnp.concatenate([far_low, far_high], 0), below])


def local(hidden_states, logit_grads, master, moment_one, moment_two):
    x, z, c = lax.axis_index("x"), lax.axis_index("zl"), lax.axis_index("c")
    dp = jnp.arange(16)
    ahead = (dp // 4 - x) % 4
    mine_z = (dp // 2 % 2 == z).astype(jnp.int32)
    mine_c = (dp % 2 == c).astype(jnp.int32)
    group = jnp.arange(96)
    slot = (((group % 6 // 3) * 2 + mine_c[group // 6]) * 8 + ahead[group // 6] * 2 + mine_z[group // 6]) * 3 + group % 3
    rel = jnp.arange(16)
    place_dp = ((x + rel % 4) % 4) * 4 + (z + rel // 4 % 2) % 2 * 2 + (c + rel // 8) % 2
    slot, place_dp = slot.astype(jnp.int32), place_dp.astype(jnp.int32)

    rows = order_rows(slot, logit_grads)
    state = (master[0], moment_one[0], moment_two[0])
    outs, head = None, None
    for half in range(2):
        for part in range(2):
            send = product(rows, hidden_states, 2 * part, half)
            keep = product(rows, hidden_states, 2 * part + 1, half)
            came = lax.ppermute(send, "c", SWAP)
            keep = keep.reshape(4, 2, ROWS, 8 * COLS)
            came = came.reshape(4, 2, ROWS, 8 * COLS)
            if part == 0:
                over = lax.ppermute((keep[:, 0] + came[:, 0]).astype(F16), "zl", SWAP)
                r = ROWS // 2
                terms = lambda k, a: (
                    keep[k, 1, a * r : a * r + r] + came[k, 1, a * r : a * r + r] + wide(over[k, a * r : a * r + r])
                )
                gradient = ring_sum(terms)
            else:
                terms = lambda k, a: keep[k, a] + came[k, a]
                total = ring_sum(terms).reshape(2, ROWS, 8 * COLS)
                over = lax.ppermute(total[0].astype(F16), "zl", SWAP)
                gradient = total[1] + wide(over)
            outs, rounded = adam(gradient, state, outs, part, half)
            mine = lax.all_to_all(rounded, ("y", "zh"), split_axis=0, concat_axis=0, tiled=True)
            if part == 0:
                row = ring_gather(mine)
                both = jnp.stack([row, lax.ppermute(row, "zl", SWAP)])
            else:
                pair = jnp.concatenate([mine, lax.ppermute(mine, "zl", SWAP)], 0)
                both = jnp.swapaxes(ring_gather(pair).reshape(4, 2, 8, ROWS, COLS), 0, 1)
            other = lax.ppermute(both, "c", SWAP)
            head = place(place_dp, both, other, head, part, half)
    return (*(o[None] for o in outs), head.reshape(12288, 512))


def solution(mesh):
    parts = Mesh(mesh.devices.reshape(4, 2, 2, 4, 2), ("x", "zl", "c", "y", "zh"))
    dp, vocab = ("x", "zl", "c"), ("y", "zh")
    held = P(vocab, dp, None)
    return jax.shard_map(
        local,
        mesh=parts,
        in_specs=(P(dp, None), P(dp, vocab), held, held, held),
        out_specs=(held, held, held, P(None, vocab)),
        check_vma=False,
    )
```

```python
import jax
import jax.numpy as jnp
from jax import lax
from jax.experimental import pallas as pl
from jax.experimental.pallas import tpu as pltpu
from jax.sharding import Mesh, PartitionSpec as P

STEP = 100

beta_one = 0.9
beta_two = 0.999
learn_rate = 0.001
decay_rate = 0.1
epsilon = 1e-08

F16 = jnp.float16
F32 = jnp.float32
BF16 = jnp.bfloat16


def params(mib):
    return pltpu.CompilerParams(vmem_limit_bytes=mib * 2**20)


SWAP = [(0, 1), (1, 0)]
UP = [(i, (i + 1) % 4) for i in range(4)]
DOWN = [(i, (i + 3) % 4) for i in range(4)]

CHUNKS = ((48, "x"), (32, "z"), (16, "x"))
GROUPS = ((0,), (1, 2))
HALF = 48


def order_kernel(where, grads, *outs):
    z, c = where[1], where[2]
    for block in range(3):
        turned = grads[:, 128 * block : 128 * block + 128].T
        for q in range(8):
            row = 128 * block + 16 * q
            owner, at = row // 96, row % 96
            keep = jnp.where(c == owner % 2, 1, 0)
            same = jnp.where(z == owner // 2, 1, 0)
            start = 0
            for (count, first), out in zip(CHUNKS, outs):
                if start <= at < start + count:
                    piece = turned[16 * q : 16 * q + 16]
                    if first == "x":
                        out[keep, 0, same, at - start : at - start + 16, :] = piece
                    else:
                        out[keep, same, 0, at - start : at - start + 16, :] = piece
                start += count


def order_rows(where, logit_grads):
    shapes, specs = [], []
    for count, first in CHUNKS:
        if first == "x":
            shapes.append((2, 4, 2, count, 2048))
            specs.append(pl.BlockSpec((2, 1, 2, count, 2048), lambda i, s: (0, i, 0, 0, 0)))
        else:
            shapes.append((2, 2, 4, count, 2048))
            specs.append(pl.BlockSpec((2, 2, 1, count, 2048), lambda i, s: (0, 0, i, 0, 0)))
    return pl.pallas_call(
        order_kernel,
        grid_spec=pltpu.PrefetchScalarGridSpec(
            num_scalar_prefetch=1,
            grid=(4,),
            in_specs=[pl.BlockSpec((2048, 384), lambda i, s: (0, (s[0] + 2 + i) % 4))],
            out_specs=specs,
        ),
        out_shape=[jax.ShapeDtypeStruct(s, BF16) for s in shapes],
        compiler_params=params(14),
        name="order_rows",
    )(where, logit_grads)


def adam_kernel(first_group, gradient, master, one, two, *rest):
    new_master, new_one, new_two, rounded = rest if first_group else rest[3:]
    g = gradient[...]
    m = beta_one * one[...] + (1.0 - beta_one) * g
    v = beta_two * two[...] + (1.0 - beta_two) * g * g
    first_hat = m / (1.0 - beta_one**STEP)
    second_hat = v / (1.0 - beta_two**STEP)
    old = master[...]
    new = old - learn_rate * (first_hat / (jnp.sqrt(second_hat) + epsilon) + decay_rate * old)
    new_master[...] = new
    new_one[...] = m
    new_two[...] = v
    rounded[0] = new[:, :512].astype(BF16)
    rounded[1] = new[:, 512:].astype(BF16)


def adam(gradient, state, outs, group):
    tile = pl.BlockSpec((HALF, 1024), lambda w: (group, w))
    given = () if outs is None else outs
    got = pl.pallas_call(
        lambda *refs: adam_kernel(outs is None, *refs),
        grid=(4,),
        in_specs=[pl.BlockSpec((HALF, 1024), lambda w: (0, w)), tile, tile, tile]
        + [pl.BlockSpec(memory_space=pl.ANY)] * len(given),
        out_specs=[tile] * 3 + [pl.BlockSpec((2, HALF, 512), lambda w: (w, 0, 0))],
        out_shape=[jax.ShapeDtypeStruct((96, 4096), F32)] * 3 + [jax.ShapeDtypeStruct((8, HALF, 512), BF16)],
        input_output_aliases={} if outs is None else {4: 0, 5: 1, 6: 2},
        compiler_params=params(6),
        name=f"adam_{group}",
    )(gradient, *state, *given)
    return got[:3], got[3]


def place(where, arrays, pieces, head, group):
    given = () if head is None else (head,)

    def kernel(where, *refs):
        out, sem = refs[-2], refs[-1]
        copies = []
        for k, (source, first, (ahead, z, c)) in enumerate(pieces):
            dp = (where[0] + ahead) % 4 * 4 + (where[1] + z) % 2 * 2 + (where[2] + c) % 2
            copies.append(
                pltpu.make_async_copy(
                    refs[source].at[pl.ds(first, 8)],
                    out.at[:, dp, pl.ds(group * HALF, HALF), :],
                    sem.at[k],
                )
            )
        for copy in copies:
            copy.start()
        for copy in copies:
            copy.wait()

    return pl.pallas_call(
        kernel,
        grid_spec=pltpu.PrefetchScalarGridSpec(
            num_scalar_prefetch=1,
            grid=(1,),
            in_specs=[pl.BlockSpec(memory_space=pl.ANY)] * (len(arrays) + len(given)),
            out_specs=pl.BlockSpec(memory_space=pl.ANY),
            scratch_shapes=[pltpu.SemaphoreType.DMA((len(pieces),))],
        ),
        out_shape=jax.ShapeDtypeStruct((8, 16, 96, 512), BF16),
        input_output_aliases={} if head is None else {1 + len(arrays): 0},
        compiler_params=params(1),
        name=f"place_{group}",
    )(where, *arrays, *given)


def wide(a):
    return a.astype(F32)


def dot(a, b):
    return jnp.dot(a, b, preferred_element_type=F32)


def ring_far(far):
    n = far.shape[0] // 2
    return lax.ppermute(far[:n], "x", UP), lax.ppermute(far[n:], "x", DOWN)


def ring_near(came, near):
    up = jnp.concatenate([near(1, 0) + wide(came[0]), near(1, 1)], 0).astype(F16)
    down = jnp.concatenate([near(3, 0), near(3, 1) + wide(came[1])], 0).astype(F16)
    return lax.ppermute(up, "x", UP), lax.ppermute(down, "x", DOWN)


def chunk_sum(rows, hidden, count, first, split):
    rows = rows.reshape(2, 8 * count, 2048)
    lead = 2 * count if first == "x" else 4 * count
    if split:
        came_lead = lax.ppermute(dot(rows[0, :lead], hidden).astype(F16), "c", SWAP)
        came_rest = lax.ppermute(dot(rows[0, lead:], hidden).astype(F16), "c", SWAP)
    else:
        came = lax.ppermute(dot(rows[0], hidden).astype(F16), "c", SWAP)
        came_lead, came_rest = came[:lead], came[lead:]
    ahead = (dot(rows[1, :lead], hidden) + wide(came_lead)).astype(F16)
    rest = dot(rows[1, lead:], hidden) + wide(came_rest)
    if first == "x":
        came = ring_far(ahead)
        at = {3: 0, 0: 2, 1: 4}
        near = lambda k, a: rest[(at[k] + a) * count : (at[k] + a + 1) * count]
        from_down, from_up = ring_near(came, near)
        over = (near(0, 0) + wide(from_down[:count]) + wide(from_up[:count])).astype(F16)
        own = near(0, 1) + wide(from_down[count:]) + wide(from_up[count:])
        return own + wide(lax.ppermute(over, "zl", SWAP))
    over = lax.ppermute(ahead, "zl", SWAP)
    n = count // 2
    at = {2: 0, 3: 2, 0: 4, 1: 6}

    def near(k, a):
        b = (at[k] + a) * n
        return rest[b : b + n] + wide(over[b : b + n])

    came = ring_far(jnp.concatenate([near(2, 0), near(2, 1)], 0).astype(F16))
    from_down, from_up = ring_near(came, near)
    own = jnp.concatenate([near(0, 0), near(0, 1)], 0)
    return own + wide(from_down) + wide(from_up)


def gather(where, mine, head, group):
    pair = jnp.concatenate([mine, lax.ppermute(mine, "zl", SWAP)], 0)
    below = lax.ppermute(pair, "x", UP)
    above = lax.ppermute(pair, "x", DOWN)
    far_low = lax.ppermute(below[:8], "x", UP)
    far_high = lax.ppermute(above[8:], "x", DOWN)
    near = jnp.concatenate([pair, above, below], 0)
    far = jnp.concatenate([far_low, far_high], 0)
    near_other = lax.ppermute(near, "c", SWAP)
    far_other = lax.ppermute(far, "c", SWAP)
    pieces = [(c, (2 * k + z) * 8, (x, z, c)) for c in range(2) for k, x in enumerate((0, 1, 3)) for z in range(2)]
    head = place(where, (near, near_other), pieces, head, group)
    pieces = [(c, z * 8, (2, z, c)) for c in range(2) for z in range(2)]
    return place(where, (far, far_other), pieces, head, group)


def local(hidden_states, logit_grads, master, moment_one, moment_two):
    where = jnp.stack([lax.axis_index("x"), lax.axis_index("zl"), lax.axis_index("c")]).astype(jnp.int32)
    rows = order_rows(where, logit_grads)
    sums = [chunk_sum(r, hidden_states, count, first, k == 0) for k, (r, (count, first)) in enumerate(zip(rows, CHUNKS))]
    state = (master[0], moment_one[0], moment_two[0])
    outs, head = None, None
    for group, members in enumerate(GROUPS):
        gradient = jnp.concatenate([sums[k] for k in members], 0)
        outs, rounded = adam(gradient, state, outs, group)
        mine = lax.all_to_all(rounded, ("y", "zh"), split_axis=0, concat_axis=0, tiled=True)
        head = gather(where, mine, head, group)
    return (*(o[None] for o in outs), head.reshape(12288, 512))


def solution(mesh):
    parts = Mesh(mesh.devices.reshape(4, 2, 2, 4, 2), ("x", "zl", "c", "y", "zh"))
    dp, vocab = ("x", "zl", "c"), ("y", "zh")
    held = P(vocab, dp, None)
    return jax.shard_map(
        local,
        mesh=parts,
        in_specs=(P(dp, None), P(dp, vocab), held, held, held),
        out_specs=(held, held, held, P(None, vocab)),
        check_vma=False,
    )
```

```python
import jax
import jax.numpy as jnp
from jax import lax
from jax.experimental import pallas as pl
from jax.experimental.pallas import tpu as pltpu
from jax.sharding import Mesh, PartitionSpec as P

STEP = 100

beta_one = 0.9
beta_two = 0.999
learn_rate = 0.001
decay_rate = 0.1
epsilon = 1e-08

F16 = jnp.float16
F32 = jnp.float32
BF16 = jnp.bfloat16


def params(mib):
    return pltpu.CompilerParams(vmem_limit_bytes=mib * 2**20)


SWAP = [(0, 1), (1, 0)]
SWAPS = [[(2 * x + c, 2 * (x ^ (1 if c == k else 3)) + c) for x in range(4) for c in range(2)] for k in range(2)]

CHUNKS = (48, 48)
STARTS = (0, 48)


def order_kernel(where, grads, *outs):
    z, c = where[1], where[2]
    for block in range(3):
        turned = grads[:, 128 * block : 128 * block + 128].T
        for q in range(8):
            row = 128 * block + 16 * q
            owner, at = row // 96, row % 96
            piece = turned[16 * q : 16 * q + 16]
            same = jnp.where(z == owner // 2, 1, 0)
            start = 0
            for k, count in enumerate(CHUNKS):
                if start <= at < start + count:
                    for keep in range(2):

                        @pl.when((c == owner % 2) == (keep == 1))
                        def _():
                            outs[2 * k + keep][0, same, at - start : at - start + 16, :] = piece

                start += count


def order_rows(where, logit_grads):
    def block(i, s):
        x, core = s[0], s[2]
        one, three = x + 1 - 2 * (x % 2), 3 - x
        first = jnp.where(core == 0, one, three)
        second = jnp.where(core == 0, three, one)
        return jnp.where(i == 0, (x + 2) % 4, jnp.where(i == 1, first, jnp.where(i == 2, second, x)))

    return pl.pallas_call(
        order_kernel,
        grid_spec=pltpu.PrefetchScalarGridSpec(
            num_scalar_prefetch=1,
            grid=(4,),
            in_specs=[pl.BlockSpec((2048, 384), lambda i, s: (0, block(i, s)))],
            out_specs=[
                pl.BlockSpec((1, 2, count, 2048), index)
                for count in CHUNKS
                for index in (
                    lambda i, s: (jnp.where((i == 1) | (i == 2), 3 - i, i), 0, 0, 0),
                    lambda i, s: (i, 0, 0, 0),
                )
            ],
        ),
        out_shape=[jax.ShapeDtypeStruct((4, 2, count, 2048), BF16) for count in CHUNKS for _ in range(2)],
        compiler_params=params(14),
        name="order_rows",
    )(where, logit_grads)


def adam_kernel(first_group, where, gradient, master, one, two, *rest):
    new_master, new_one, new_two, rounded = rest if first_group else rest[3:]
    g = gradient[...]
    m = beta_one * one[...] + (1.0 - beta_one) * g
    v = beta_two * two[...] + (1.0 - beta_two) * g * g
    first_hat = m / (1.0 - beta_one**STEP)
    second_hat = v / (1.0 - beta_two**STEP)
    old = master[...]
    new = old - learn_rate * (first_hat / (jnp.sqrt(second_hat) + epsilon) + decay_rate * old)
    new_master[...] = new
    new_one[...] = m
    new_two[...] = v
    rounded[where[4], 0] = new[:, :512].astype(BF16)
    rounded[1 - where[4], 0] = new[:, 512:].astype(BF16)


def adam(where, gradient, state, outs, group):
    rows, at = CHUNKS[group], STARTS[group] // CHUNKS[group]
    tile = pl.BlockSpec((rows, 1024), lambda w, s: (at, w))
    given = () if outs is None else outs
    got = pl.pallas_call(
        lambda *refs: adam_kernel(outs is None, *refs),
        grid_spec=pltpu.PrefetchScalarGridSpec(
            num_scalar_prefetch=1,
            grid=(4,),
            in_specs=[pl.BlockSpec((rows, 1024), lambda w, s: (0, w)), tile, tile, tile]
            + [pl.BlockSpec(memory_space=pl.ANY)] * len(given),
            out_specs=[tile] * 3 + [pl.BlockSpec((2, 1, rows, 512), lambda w, s: (0, (w + 4 - s[3]) % 4, 0, 0))],
        ),
        out_shape=[jax.ShapeDtypeStruct((96, 4096), F32)] * 3 + [jax.ShapeDtypeStruct((2, 4, rows, 512), BF16)],
        input_output_aliases={} if outs is None else {5: 0, 6: 1, 7: 2},
        compiler_params=params(6),
        name=f"adam_{group}",
    )(where, gradient, *state, *given)
    return got[:3], got[3]


def exchange(where, rounded, gate):
    rows = rounded.shape[2]
    got = after(lax.ppermute(rounded[1], "zh", SWAP), *gate)
    came = [
        lax.ppermute(jnp.stack([rounded[0, k], got[k]]), "y", [(i, (i + k) % 4) for i in range(4)]) for k in (1, 2, 3)
    ]

    def kernel(where, rounded, got, one, two, three, out, sem):
        copies = []
        for k, pair in enumerate(((rounded.at[0, 0], got.at[0]), *((a.at[0], a.at[1]) for a in (one, two, three)))):
            for r, source in enumerate(pair):
                block = (where[3] + 4 - k) % 4 * 2 + (where[4] + r) % 2
                copies.append(pltpu.make_async_copy(source, out.at[block], sem.at[2 * k + r]))
        for copy in copies:
            copy.start()
        for copy in copies:
            copy.wait()

    whole = pl.BlockSpec(memory_space=pl.ANY)
    return pl.pallas_call(
        kernel,
        grid_spec=pltpu.PrefetchScalarGridSpec(
            num_scalar_prefetch=1,
            grid=(1,),
            in_specs=[whole] * 5,
            out_specs=whole,
            scratch_shapes=[pltpu.SemaphoreType.DMA((8,))],
        ),
        out_shape=jax.ShapeDtypeStruct((8, rows, 512), BF16),
        compiler_params=params(1),
        name="collect",
    )(where, rounded, got, *came)


def place(where, arrays, pieces, head, group):
    given = () if head is None else (head,)

    def kernel(where, *refs):
        out, mark, sem = refs[-3:]
        copies = []
        x = where[0]
        one, three = x + 1 - 2 * (x % 2), 3 - x
        for k, (source, first, (at, z, c)) in enumerate(pieces):
            core = (where[2] + c) % 2
            from_x = (x, jnp.where(core == 0, three, one), jnp.where(core == 0, one, three), (x + 2) % 4)[at]
            dp = from_x * 4 + (where[1] + z) % 2 * 2 + core
            copies.append(
                pltpu.make_async_copy(
                    refs[source].at[pl.ds(first, 8)],
                    out.at[:, dp, pl.ds(STARTS[group], CHUNKS[group]), :],
                    sem.at[k],
                )
            )
        for copy in copies:
            copy.start()
        mark[...] = jnp.zeros_like(mark)
        for copy in copies:
            copy.wait()

    whole = pl.BlockSpec(memory_space=pl.ANY)
    return pl.pallas_call(
        kernel,
        grid_spec=pltpu.PrefetchScalarGridSpec(
            num_scalar_prefetch=1,
            grid=(1,),
            in_specs=[whole] * (len(arrays) + len(given)),
            out_specs=[whole, pl.BlockSpec((8, 128), lambda i, s: (0, 0))],
            scratch_shapes=[pltpu.SemaphoreType.DMA((len(pieces),))],
        ),
        out_shape=[jax.ShapeDtypeStruct((8, 16, 96, 512), BF16), jax.ShapeDtypeStruct((8, 128), F32)],
        input_output_aliases={} if head is None else {1 + len(arrays): 0},
        compiler_params=params(1),
        name=f"place_{group}",
    )(where, *arrays, *given)


def after(value, *others):
    if not others:
        return value

    def kernel(*refs):
        pass

    others = [a[:8, :128].astype(F32) if a.dtype == F16 else a for a in others]
    whole = pl.BlockSpec(memory_space=pl.ANY)
    return pl.pallas_call(
        kernel,
        in_specs=[whole] * (1 + len(others)),
        out_specs=whole,
        out_shape=jax.ShapeDtypeStruct(value.shape, value.dtype),
        input_output_aliases={0: 0},
        compiler_params=params(1),
        name="after",
    )(value, *others)


def wide(a):
    return a.astype(F32)


def dot(a, b):
    return jnp.dot(a, b, preferred_element_type=F32)


def swap(a, k):
    return lax.ppermute(a, ("x", "c"), SWAPS[k])


def gather(where, mine, head, group, marks, gate):
    side = lax.ppermute(mine, "zl", SWAP)
    for z, own in enumerate((mine, side)):
        pair = jnp.concatenate([own, swap(own, 1)], 0)
        far = swap(after(pair, *gate) if z == 0 else pair, 0)
        for at, a in ((0, pair), (2, far)):
            if group == 1 and z == 1 and at == 2:
                a = after(a, *marks)
            pieces = [(c, 8 * k, (at + k, z, c)) for c in range(2) for k in range(2)]
            head, mark = place(where, (a, lax.ppermute(a, "c", SWAP)), pieces, head, group)
            marks = marks + [mark]
    return head, marks, pair


def local(hidden_states, logit_grads, master, moment_one, moment_two):
    where = jnp.stack([lax.axis_index(a) for a in ("x", "zl", "c", "y", "zh")]).astype(jnp.int32)
    rows = order_rows(where, logit_grads)
    rows = [a.reshape(-1, 2048) for a in rows]

    def send_first(keep, came):
        n = keep.shape[0] // 2
        sent = (keep[:n] + wide(came[:n])).astype(F16)
        return swap(sent, 0), sent

    def send_second(keep, came, got, after_this):
        n = keep.shape[0] // 4
        total = keep[2 * n : 3 * n] + wide(came[2 * n : 3 * n]) + wide(got[:n])
        if after_this is not None:
            total = total + after_this.reshape(-1)[:1].astype(F32)[:, None] * 0
        sent = total.astype(F16)
        return swap(sent, 1), sent

    def send_side(keep, came, got, last):
        n = keep.shape[0] // 4
        own = keep[3 * n :] + wide(came[3 * n :]) + wide(got[n:]) + wide(last)
        return own[n // 2 :] + wide(lax.ppermute(own[: n // 2].astype(F16), "zl", SWAP)), own

    def update(gradient, outs, group, gate):
        outs, rounded = adam(where, gradient, (master[0], moment_one[0], moment_two[0]), outs, group)
        return outs, exchange(where, rounded, gate)

    came_a = lax.ppermute(dot(rows[0], hidden_states).astype(F16), "c", SWAP)
    keep_a = dot(rows[1], hidden_states)
    first_a, _ = send_first(keep_a, came_a)
    came_b = lax.ppermute(dot(after(rows[2], keep_a), hidden_states).astype(F16), "c", SWAP)
    second_a, sent = send_second(keep_a, came_a, first_a, None)
    keep_b = dot(after(rows[3], sent), hidden_states)
    first_b, sent = send_first(keep_b, came_b)
    gradient, _ = send_side(keep_a, came_a, first_a, second_a)
    outs, mine = update(after(gradient, sent), None, 0, ())
    second_b, _ = send_second(keep_b, came_b, first_b, None)
    gradient, own = send_side(keep_b, came_b, first_b, second_b)
    head, marks, pair = gather(where, mine, None, 0, [], (own,))
    outs, mine = update(gradient, outs, 1, (pair,))
    head, _, _ = gather(where, mine, head, 1, marks, ())
    return (*(o[None] for o in outs), head.reshape(12288, 512))


def solution(mesh):
    parts = Mesh(mesh.devices.reshape(4, 2, 2, 4, 2), ("x", "zl", "c", "y", "zh"))
    dp, vocab = ("x", "zl", "c"), ("y", "zh")
    held = P(vocab, dp, None)
    return jax.shard_map(
        local,
        mesh=parts,
        in_specs=(P(dp, None), P(dp, vocab), held, held, held),
        out_specs=(held, held, held, P(None, vocab)),
        check_vma=False,
    )
```

```python
import jax
import jax.numpy as jnp
from jax import lax
from jax.experimental import pallas as pl
from jax.experimental.pallas import tpu as pltpu
from jax.sharding import Mesh, PartitionSpec as P

STEP = 100

beta_one = 0.9
beta_two = 0.999
learn_rate = 0.001
decay_rate = 0.1
epsilon = 1e-08

F16 = jnp.float16
F32 = jnp.float32
BF16 = jnp.bfloat16


def params(mib):
    return pltpu.CompilerParams(vmem_limit_bytes=mib * 2**20)


SWAP = [(0, 1), (1, 0)]
SWAPS = [[(2 * x + c, 2 * (x ^ (1 if c == k else 3)) + c) for x in range(4) for c in range(2)] for k in range(2)]

CHUNKS = (48, 48)
STARTS = (0, 48)


def order_kernel(where, grads, *outs):
    z, c = where[1], where[2]
    for block in range(3):
        turned = grads[:, 128 * block : 128 * block + 128].T
        for q in range(8):
            row = 128 * block + 16 * q
            owner, at = row // 96, row % 96
            piece = turned[16 * q : 16 * q + 16]
            same = jnp.where(z == owner // 2, 1, 0)
            for k, (start, count) in enumerate(zip(STARTS, CHUNKS)):
                if start <= at < start + count:
                    for keep in range(2):

                        @pl.when((c == owner % 2) == (keep == 1))
                        def _():
                            outs[2 * k + keep][0, same, at - start : at - start + 16, :] = piece


def order_rows(where, logit_grads):
    def block(i, s):
        x, core = s[0], s[2]
        one, three = x + 1 - 2 * (x % 2), 3 - x
        first = jnp.where(core == 0, one, three)
        second = jnp.where(core == 0, three, one)
        return jnp.where(i == 0, (x + 2) % 4, jnp.where(i == 1, first, jnp.where(i == 2, second, x)))

    return pl.pallas_call(
        order_kernel,
        grid_spec=pltpu.PrefetchScalarGridSpec(
            num_scalar_prefetch=1,
            grid=(4,),
            in_specs=[pl.BlockSpec((2048, 384), lambda i, s: (0, block(i, s)))],
            out_specs=[
                pl.BlockSpec((1, 2, count, 2048), index)
                for count in CHUNKS
                for index in (
                    lambda i, s: (jnp.where((i == 1) | (i == 2), 3 - i, i), 0, 0, 0),
                    lambda i, s: (i, 0, 0, 0),
                )
            ],
        ),
        out_shape=[jax.ShapeDtypeStruct((4, 2, count, 2048), BF16) for count in CHUNKS for _ in range(2)],
        compiler_params=params(14),
        name="order_rows",
    )(where, logit_grads)


def adam_kernel(first_group, where, gradient, master, one, two, *rest):
    new_master, new_one, new_two, rounded = rest if first_group else rest[3:]
    g = gradient[...]
    m = beta_one * one[...] + (1.0 - beta_one) * g
    v = beta_two * two[...] + (1.0 - beta_two) * g * g
    first_hat = m / (1.0 - beta_one**STEP)
    second_hat = v / (1.0 - beta_two**STEP)
    old = master[...]
    new = old - learn_rate * (first_hat / (jnp.sqrt(second_hat) + epsilon) + decay_rate * old)
    new_master[...] = new
    new_one[...] = m
    new_two[...] = v
    rounded[where[4], 0] = new[:, :512].astype(BF16)
    rounded[1 - where[4], 0] = new[:, 512:].astype(BF16)


def adam(where, gradient, state, outs, group):
    rows, at = CHUNKS[group], STARTS[group] // CHUNKS[group]
    tile = pl.BlockSpec((rows, 1024), lambda w, s: (at, w))
    given = () if outs is None else outs
    got = pl.pallas_call(
        lambda *refs: adam_kernel(outs is None, *refs),
        grid_spec=pltpu.PrefetchScalarGridSpec(
            num_scalar_prefetch=1,
            grid=(4,),
            in_specs=[pl.BlockSpec((rows, 1024), lambda w, s: (0, w)), tile, tile, tile]
            + [pl.BlockSpec(memory_space=pl.ANY)] * len(given),
            out_specs=[tile] * 3 + [pl.BlockSpec((2, 1, rows, 512), lambda w, s: (0, (w + 4 - s[3]) % 4, 0, 0))],
        ),
        out_shape=[jax.ShapeDtypeStruct((96, 4096), F32)] * 3 + [jax.ShapeDtypeStruct((2, 4, rows, 512), BF16)],
        input_output_aliases={} if outs is None else {5: 0, 6: 1, 7: 2},
        compiler_params=params(6),
        name=f"adam_{group}",
    )(where, gradient, *state, *given)
    return got[:3], got[3]


def exchange(where, rounded, gate):
    rows = rounded.shape[2]
    got = after(lax.ppermute(rounded[1], "zh", SWAP), *gate)
    came = [
        lax.ppermute(jnp.stack([rounded[0, k], got[k]]), "y", [(i, (i + k) % 4) for i in range(4)]) for k in (1, 2, 3)
    ]

    def kernel(where, rounded, got, one, two, three, out, sem):
        copies = []
        for k, pair in enumerate(((rounded.at[0, 0], got.at[0]), *((a.at[0], a.at[1]) for a in (one, two, three)))):
            for r, source in enumerate(pair):
                block = (where[3] + 4 - k) % 4 * 2 + (where[4] + r) % 2
                copies.append(pltpu.make_async_copy(source, out.at[block], sem.at[2 * k + r]))
        for copy in copies:
            copy.start()
        for copy in copies:
            copy.wait()

    whole = pl.BlockSpec(memory_space=pl.ANY)
    return pl.pallas_call(
        kernel,
        grid_spec=pltpu.PrefetchScalarGridSpec(
            num_scalar_prefetch=1,
            grid=(1,),
            in_specs=[whole] * 5,
            out_specs=whole,
            scratch_shapes=[pltpu.SemaphoreType.DMA((8,))],
        ),
        out_shape=jax.ShapeDtypeStruct((8, rows, 512), BF16),
        compiler_params=params(1),
        name="collect",
    )(where, rounded, got, *came)


def place(where, arrays, pieces, head, group, others=()):
    given = (*others, *(() if head is None else (head,)))

    def kernel(where, *refs):
        out, mark, sem = refs[-3:]
        copies = []
        x = where[0]
        one, three = x + 1 - 2 * (x % 2), 3 - x
        for k, (source, first, (at, z, c)) in enumerate(pieces):
            core = (where[2] + c) % 2
            from_x = (x, jnp.where(core == 0, three, one), jnp.where(core == 0, one, three), (x + 2) % 4)[at]
            dp = from_x * 4 + (where[1] + z) % 2 * 2 + core
            copies.append(
                pltpu.make_async_copy(
                    refs[source].at[pl.ds(first, 8)],
                    out.at[:, dp, pl.ds(STARTS[group], CHUNKS[group]), :],
                    sem.at[k],
                )
            )
        for copy in copies:
            copy.start()
        mark[...] = jnp.zeros_like(mark)
        for copy in copies:
            copy.wait()

    whole = pl.BlockSpec(memory_space=pl.ANY)
    return pl.pallas_call(
        kernel,
        grid_spec=pltpu.PrefetchScalarGridSpec(
            num_scalar_prefetch=1,
            grid=(1,),
            in_specs=[whole] * (len(arrays) + len(given)),
            out_specs=[whole, pl.BlockSpec((8, 128), lambda i, s: (0, 0))],
            scratch_shapes=[pltpu.SemaphoreType.DMA((len(pieces),))],
        ),
        out_shape=[jax.ShapeDtypeStruct((8, 16, 96, 512), BF16), jax.ShapeDtypeStruct((8, 128), F32)],
        input_output_aliases={} if head is None else {len(arrays) + len(given): 0},
        compiler_params=params(1),
        name=f"place_{group}",
    )(where, *arrays, *given)


def after(value, *others):
    if not others:
        return value

    def kernel(*refs):
        pass

    others = [a[:8, :128].astype(F32) if a.dtype == F16 else a for a in others]
    whole = pl.BlockSpec(memory_space=pl.ANY)
    return pl.pallas_call(
        kernel,
        in_specs=[whole] * (1 + len(others)),
        out_specs=whole,
        out_shape=jax.ShapeDtypeStruct(value.shape, value.dtype),
        input_output_aliases={0: 0},
        compiler_params=params(1),
        name="after",
    )(value, *others)


def wide(a):
    return a.astype(F32)


def dot(a, b):
    return jnp.dot(a, b, preferred_element_type=F32)


def swap(a, k):
    return lax.ppermute(a, ("x", "c"), SWAPS[k])


def gather(mine, gate):
    side = lax.ppermute(mine, "zl", SWAP)
    pairs, fars = [], []
    for z, own in enumerate((mine, side)):
        pairs.append(jnp.concatenate([own, swap(own, 1)], 0))
        fars.append(swap(after(pairs[z], *gate) if z == 0 else pairs[z], 0))
    return pairs, fars


def place_all(where, chains, head, group, others=()):
    arrays, pieces = [], []
    for a, at, z in chains:
        for c, source in enumerate((a, lax.ppermute(a, "c", SWAP))):
            pieces += [(len(arrays), 8 * k, (at + k, z, c)) for k in range(2)]
            arrays.append(source)
    return place(where, arrays, pieces, head, group, others)


def local(hidden_states, logit_grads, master, moment_one, moment_two):
    where = jnp.stack([lax.axis_index(a) for a in ("x", "zl", "c", "y", "zh")]).astype(jnp.int32)
    rows = order_rows(where, logit_grads)
    rows = [a.reshape(-1, 2048) for a in rows]

    def send_first(keep, came):
        n = keep.shape[0] // 2
        sent = (keep[:n] + wide(came[:n])).astype(F16)
        return swap(sent, 0), sent

    def send_second(keep, came, got, after_this):
        n = keep.shape[0] // 4
        total = keep[2 * n : 3 * n] + wide(came[2 * n : 3 * n]) + wide(got[:n])
        if after_this is not None:
            total = total + after_this.astype(F32) * 0
        sent = total.astype(F16)
        return swap(sent, 1), sent

    def send_side(keep, came, got, last):
        n = keep.shape[0] // 4
        own = keep[3 * n :] + wide(came[3 * n :]) + wide(got[n:]) + wide(last)
        return own[n // 2 :] + wide(lax.ppermute(own[: n // 2].astype(F16), "zl", SWAP)), own

    def update(gradient, outs, group, gate):
        outs, rounded = adam(where, gradient, (master[0], moment_one[0], moment_two[0]), outs, group)
        return outs, exchange(where, rounded, gate), rounded[0, 0, :1, :1]

    came_a = lax.ppermute(dot(rows[0], hidden_states).astype(F16), "c", SWAP)
    keep_a = dot(rows[1], hidden_states)
    first_a, _ = send_first(keep_a, came_a)
    came_b = lax.ppermute(dot(after(rows[2], keep_a), hidden_states).astype(F16), "c", SWAP)
    second_a, sent = send_second(keep_a, came_a, first_a, None)
    keep_b = dot(after(rows[3], sent), hidden_states)
    first_b, sent = send_first(keep_b, came_b)
    gradient, _ = send_side(keep_a, came_a, first_a, second_a)
    outs, mine, done = update(after(gradient, sent), None, 0, ())
    second_b, _ = send_second(keep_b, came_b, first_b, done)
    gradient, own = send_side(keep_b, came_b, first_b, second_b)
    pairs_a, fars_a = gather(after(mine, own), ())
    outs, mine, _ = update(after(gradient, pairs_a[0]), outs, 1, (pairs_a[1],))
    pairs_b, fars_b = gather(after(mine, fars_a[0]), (fars_a[1],))
    chains = [(a, at, z) for z in range(2) for a, at in ((pairs_a[z], 0), (fars_a[z], 2))]
    head, _ = place_all(where, chains, None, 0, (pairs_b[1],))
    head, mark = place_all(where, [(pairs_b[0], 0, 0), (fars_b[0], 2, 0), (pairs_b[1], 0, 1)], head, 1)
    head, _ = place_all(where, [(after(fars_b[1], mark), 2, 1)], head, 1)
    return (*(o[None] for o in outs), head.reshape(12288, 512))


def solution(mesh):
    parts = Mesh(mesh.devices.reshape(4, 2, 2, 4, 2), ("x", "zl", "c", "y", "zh"))
    dp, vocab = ("x", "zl", "c"), ("y", "zh")
    held = P(vocab, dp, None)
    return jax.shard_map(
        local,
        mesh=parts,
        in_specs=(P(dp, None), P(dp, vocab), held, held, held),
        out_specs=(held, held, held, P(None, vocab)),
        check_vma=False,
    )
```

```python
import jax
import jax.numpy as jnp
from jax import lax
from jax.experimental import pallas as pl
from jax.experimental.pallas import tpu as pltpu
from jax.sharding import Mesh, PartitionSpec as P

STEP = 100

beta_one = 0.9
beta_two = 0.999
learn_rate = 0.001
decay_rate = 0.1
epsilon = 1e-08

F16 = jnp.float16
F32 = jnp.float32
BF16 = jnp.bfloat16


def params(mib):
    return pltpu.CompilerParams(vmem_limit_bytes=mib * 2**20)


SWAP = [(0, 1), (1, 0)]
SWAPS = [[(2 * x + c, 2 * (x ^ (1 if c == k else 3)) + c) for x in range(4) for c in range(2)] for k in range(2)]

CHUNKS = (48, 48)
STARTS = (0, 48)


def order_kernel(where, grads, *outs):
    z, c = where[1], where[2]
    for block in range(3):
        turned = grads[:, 128 * block : 128 * block + 128].T
        for q in range(8):
            row = 128 * block + 16 * q
            owner, at = row // 96, row % 96
            piece = turned[16 * q : 16 * q + 16]
            same = jnp.where(z == owner // 2, 1, 0)
            for k, (start, count) in enumerate(zip(STARTS, CHUNKS)):
                if start <= at < start + count:
                    for keep in range(2):

                        @pl.when((c == owner % 2) == (keep == 1))
                        def _():
                            outs[2 * k + keep][0, same, at - start : at - start + 16, :] = piece


def order_rows(where, logit_grads):
    def block(i, s):
        x, core = s[0], s[2]
        one, three = x + 1 - 2 * (x % 2), 3 - x
        first = jnp.where(core == 0, one, three)
        second = jnp.where(core == 0, three, one)
        return jnp.where(i == 0, (x + 2) % 4, jnp.where(i == 1, first, jnp.where(i == 2, second, x)))

    return pl.pallas_call(
        order_kernel,
        grid_spec=pltpu.PrefetchScalarGridSpec(
            num_scalar_prefetch=1,
            grid=(4,),
            in_specs=[pl.BlockSpec((2048, 384), lambda i, s: (0, block(i, s)))],
            out_specs=[
                pl.BlockSpec((1, 2, count, 2048), index)
                for count in CHUNKS
                for index in (
                    lambda i, s: (jnp.where((i == 1) | (i == 2), 3 - i, i), 0, 0, 0),
                    lambda i, s: (i, 0, 0, 0),
                )
            ],
        ),
        out_shape=[jax.ShapeDtypeStruct((4, 2, count, 2048), BF16) for count in CHUNKS for _ in range(2)],
        compiler_params=params(48),
        name="order_rows",
    )(where, logit_grads)


def adam_kernel(first_group, where, gradient, master, one, two, *rest):
    new_master, new_one, new_two, rounded = rest if first_group else rest[3:]
    g = gradient[...]
    m = beta_one * one[...] + (1.0 - beta_one) * g
    v = beta_two * two[...] + (1.0 - beta_two) * g * g
    first_hat = m / (1.0 - beta_one**STEP)
    second_hat = v / (1.0 - beta_two**STEP)
    old = master[...]
    new = old - learn_rate * (first_hat / (jnp.sqrt(second_hat) + epsilon) + decay_rate * old)
    new_master[...] = new
    new_one[...] = m
    new_two[...] = v
    rounded[where[4], 0] = new[:, :512].astype(BF16)
    rounded[1 - where[4], 0] = new[:, 512:].astype(BF16)


def adam(where, gradient, state, outs, group):
    rows, at = CHUNKS[group], STARTS[group] // CHUNKS[group]
    tile = pl.BlockSpec((rows, 1024), lambda w, s: (at, w))
    given = () if outs is None else outs
    got = pl.pallas_call(
        lambda *refs: adam_kernel(outs is None, *refs),
        grid_spec=pltpu.PrefetchScalarGridSpec(
            num_scalar_prefetch=1,
            grid=(4,),
            in_specs=[pl.BlockSpec((rows, 1024), lambda w, s: (0, w)), tile, tile, tile]
            + [pl.BlockSpec(memory_space=pl.ANY)] * len(given),
            out_specs=[tile] * 3 + [pl.BlockSpec((2, 1, rows, 512), lambda w, s: (0, (w + 4 - s[3]) % 4, 0, 0))],
        ),
        out_shape=[jax.ShapeDtypeStruct((96, 4096), F32)] * 3 + [jax.ShapeDtypeStruct((2, 4, rows, 512), BF16)],
        input_output_aliases={} if outs is None else {5: 0, 6: 1, 7: 2},
        compiler_params=params(6),
        name=f"adam_{group}",
    )(where, gradient, *state, *given)
    return got[:3], got[3]


def exchange(where, rounded, gate):
    rows = rounded.shape[2]
    got = after(lax.ppermute(rounded[1], "zh", SWAP), *gate)
    came = [
        lax.ppermute(jnp.stack([rounded[0, k], got[k]]), "y", [(i, (i + k) % 4) for i in range(4)]) for k in (1, 2, 3)
    ]

    def kernel(where, rounded, got, one, two, three, out, sem):
        copies = []
        for k, pair in enumerate(((rounded.at[0, 0], got.at[0]), *((a.at[0], a.at[1]) for a in (one, two, three)))):
            for r, source in enumerate(pair):
                block = (where[3] + 4 - k) % 4 * 2 + (where[4] + r) % 2
                copies.append(pltpu.make_async_copy(source, out.at[block], sem.at[2 * k + r]))
        for copy in copies:
            copy.start()
        for copy in copies:
            copy.wait()

    whole = pl.BlockSpec(memory_space=pl.ANY)
    return pl.pallas_call(
        kernel,
        grid_spec=pltpu.PrefetchScalarGridSpec(
            num_scalar_prefetch=1,
            grid=(1,),
            in_specs=[whole] * 5,
            out_specs=whole,
            scratch_shapes=[pltpu.SemaphoreType.DMA((8,))],
        ),
        out_shape=jax.ShapeDtypeStruct((8, rows, 512), BF16),
        compiler_params=params(1),
        name="collect",
    )(where, rounded, got, *came)


def place(where, arrays, pieces, head, group, others=()):
    given = (*others, *(() if head is None else (head,)))

    def kernel(where, *refs):
        out, mark, sem = refs[-3:]
        copies = []
        x = where[0]
        one, three = x + 1 - 2 * (x % 2), 3 - x
        for k, (source, first, (at, z, c)) in enumerate(pieces):
            core = (where[2] + c) % 2
            from_x = (x, jnp.where(core == 0, three, one), jnp.where(core == 0, one, three), (x + 2) % 4)[at]
            dp = from_x * 4 + (where[1] + z) % 2 * 2 + core
            copies.append(
                pltpu.make_async_copy(
                    refs[source].at[pl.ds(first, 8)],
                    out.at[:, dp, pl.ds(STARTS[group], CHUNKS[group]), :],
                    sem.at[k],
                )
            )
        for copy in copies:
            copy.start()
        mark[...] = jnp.zeros_like(mark)
        for copy in copies:
            copy.wait()

    whole = pl.BlockSpec(memory_space=pl.ANY)
    return pl.pallas_call(
        kernel,
        grid_spec=pltpu.PrefetchScalarGridSpec(
            num_scalar_prefetch=1,
            grid=(1,),
            in_specs=[whole] * (len(arrays) + len(given)),
            out_specs=[whole, pl.BlockSpec((8, 128), lambda i, s: (0, 0))],
            scratch_shapes=[pltpu.SemaphoreType.DMA((len(pieces),))],
        ),
        out_shape=[jax.ShapeDtypeStruct((8, 16, 96, 512), BF16), jax.ShapeDtypeStruct((8, 128), F32)],
        input_output_aliases={} if head is None else {len(arrays) + len(given): 0},
        compiler_params=params(1),
        name=f"place_{group}",
    )(where, *arrays, *given)


def after(value, *others):
    if not others:
        return value

    def kernel(*refs):
        pass

    others = [a[:8, :128].astype(F32) if a.dtype == F16 else a for a in others]
    whole = pl.BlockSpec(memory_space=pl.ANY)
    return pl.pallas_call(
        kernel,
        in_specs=[whole] * (1 + len(others)),
        out_specs=whole,
        out_shape=jax.ShapeDtypeStruct(value.shape, value.dtype),
        input_output_aliases={0: 0},
        compiler_params=params(1),
        name="after",
    )(value, *others)


def wide(a):
    return a.astype(F32)


def dot(a, b):
    return jnp.dot(a, b, preferred_element_type=F32)


def swap(a, k):
    return lax.ppermute(a, ("x", "c"), SWAPS[k])


def gather(mine, gate):
    side = lax.ppermute(mine, "zl", SWAP)
    pairs, fars = [], []
    for z, own in enumerate((mine, side)):
        pairs.append(jnp.concatenate([own, swap(own, 1)], 0))
        fars.append(swap(after(pairs[z], *gate) if z == 0 else pairs[z], 0))
    return pairs, fars


def place_all(where, chains, head, group, others=()):
    arrays, pieces = [], []
    for a, at, z in chains:
        for c, source in enumerate((a, lax.ppermute(a, "c", SWAP))):
            pieces += [(len(arrays), 8 * k, (at + k, z, c)) for k in range(2)]
            arrays.append(source)
    return place(where, arrays, pieces, head, group, others)


def local(hidden_states, logit_grads, master, moment_one, moment_two):
    where = jnp.stack([lax.axis_index(a) for a in ("x", "zl", "c", "y", "zh")]).astype(jnp.int32)
    rows = order_rows(where, logit_grads)
    rows = [a.reshape(-1, 2048) for a in rows]

    def send_first(keep, came):
        n = keep.shape[0] // 2
        sent = (keep[:n] + wide(came[:n])).astype(F16)
        return swap(sent, 0), sent

    def send_second(keep, came, got, after_this):
        n = keep.shape[0] // 4
        total = keep[2 * n : 3 * n] + wide(came[2 * n : 3 * n]) + wide(got[:n])
        if after_this is not None:
            total = total + after_this.astype(F32) * 0
        sent = total.astype(F16)
        return swap(sent, 1), sent

    def send_side(keep, came, got, last):
        n = keep.shape[0] // 4
        own = keep[3 * n :] + wide(came[3 * n :]) + wide(got[n:]) + wide(last)
        return own[n // 2 :] + wide(lax.ppermute(own[: n // 2].astype(F16), "zl", SWAP)), own

    def update(gradient, outs, group, gate):
        outs, rounded = adam(where, gradient, (master[0], moment_one[0], moment_two[0]), outs, group)
        return outs, exchange(where, rounded, gate), rounded[0, 0, :1, :1]

    came_a = lax.ppermute(dot(rows[0], hidden_states).astype(F16), "c", SWAP)
    keep_a = dot(rows[1], hidden_states)
    first_a, _ = send_first(keep_a, came_a)
    came_b = lax.ppermute(dot(after(rows[2], keep_a), hidden_states).astype(F16), "c", SWAP)
    second_a, sent = send_second(keep_a, came_a, first_a, None)
    keep_b = dot(after(rows[3], sent), hidden_states)
    first_b, sent = send_first(keep_b, came_b)
    gradient, _ = send_side(keep_a, came_a, first_a, second_a)
    outs, mine, done = update(after(gradient, sent), None, 0, ())
    second_b, _ = send_second(keep_b, came_b, first_b, done)
    gradient, own = send_side(keep_b, came_b, first_b, second_b)
    pairs_a, fars_a = gather(after(mine, own), ())
    outs, mine, _ = update(after(gradient, pairs_a[0]), outs, 1, (pairs_a[1],))
    pairs_b, fars_b = gather(after(mine, fars_a[0]), (fars_a[1],))
    chains = [(a, at, z) for z in range(2) for a, at in ((pairs_a[z], 0), (fars_a[z], 2))]
    head, _ = place_all(where, chains, None, 0, (pairs_b[1],))
    head, mark = place_all(where, [(pairs_b[0], 0, 0), (fars_b[0], 2, 0), (pairs_b[1], 0, 1)], head, 1)
    head, _ = place_all(where, [(after(fars_b[1], mark), 2, 1)], head, 1)
    return (*(o[None] for o in outs), head.reshape(12288, 512))


def solution(mesh):
    parts = Mesh(mesh.devices.reshape(4, 2, 2, 4, 2), ("x", "zl", "c", "y", "zh"))
    dp, vocab = ("x", "zl", "c"), ("y", "zh")
    held = P(vocab, dp, None)
    return jax.shard_map(
        local,
        mesh=parts,
        in_specs=(P(dp, None), P(dp, vocab), held, held, held),
        out_specs=(held, held, held, P(None, vocab)),
        check_vma=False,
    )
```
